32 devices in a mesh: section: 4 (over x, core), expert: 8 (over z, y).
Axes of the slice: x: 2, y: 2, z: 4, core: 2. Of those that a mesh axis runs over, the one named last changes fastest.
Arguments:
- inputs: bfloat16 [4, 2, 512, 2048], P('section', None, 'expert'), may hold values from -6 to 6
- routes: int32 [4, 2, 512, 10], P('section', None, 'expert'), may hold values from 0 to 15, all different within a row; in each aligned block of 64 rows (0 to 63, 64 to 127, ..., all dimensions but the last counted through in order) at most 48 rows name the same one
- gates: float32 [4, 2, 512, 10], P('section', None, 'expert'), may hold values from 0.1 to 0.6
- cot_early: bfloat16 [4, 512, 2048], P('section', 'expert'), may hold values from -6 to 6
- head_grad: bfloat16 [512, 2048], P('expert'), may hold values from -6 to 6
- w_gate: bfloat16 [4, 16, 2048, 512], P('section', 'expert'), may hold values from -0.125 to 0.125
- w_up: bfloat16 [4, 16, 2048, 512], P('section', 'expert'), may hold values from -0.125 to 0.125
- w_down: bfloat16 [4, 16, 512, 2048], P('section', 'expert'), may hold values from -0.25 to 0.25
Outputs:
- grad_early: bfloat16 [4, 512, 2048], P('section', 'expert')
- grad_late: bfloat16 [4, 512, 2048], P('section', 'expert')
- grad_gate: bfloat16 [4, 16, 2048, 512], P('section', 'expert')
- grad_up: bfloat16 [4, 16, 2048, 512], P('section', 'expert')
- grad_down: bfloat16 [4, 16, 512, 2048], P('section', 'expert')
The draws below stay inside these ranges and needn't reach their ends.
Inputs may be any that keep to these rules, and one draw needn't show every extreme that they name: `routes`: each row names 10 different experts. In each aligned block of 64 rows (one device's tokens of one micro-batch at one section) no expert is named by more than 48 rows, a bound that some block reaches.
All inputs are finite; a program needn't handle non-finite values.
Results may differ from the reference program's by a relative error of at most 0.008.
Values may be sent and summed in bfloat16 or wider, within the bound.
No kernel may reach another device: no remote copies, remote signals or barrier semaphores. Data moves between devices by JAX's collectives and lax.ppermute only.
A program may use at most 128 MiB of HBM per device.

```python
import math
import jax
import jax.numpy as jnp
import numpy as np
from jax import lax

D = 2048
FF_E = 512
TOPK = 10
EXPERTS = 16
TOK_DEV = 64
CAP = 48
TOKENS = 512
SECTIONS = 4
N_EXPERT = 8


def steps_of(rng, shape, cuts, smallest, high):
    loudness, own = 1.0, jax.random.fold_in(rng, 6)
    for axis_at, parts in cuts:
        draws = jnp.exp(jax.random.uniform(jax.random.fold_in(own, axis_at), (parts,), jnp.float32, smallest / len(cuts), high / len(cuts)))
        loudness = loudness * jnp.repeat(draws, shape[axis_at] // parts).reshape([-1 if axis == axis_at else 1 for axis in range(len(shape))])
    return loudness


def assign_block(rng, own, number, rows, number_of, top, limit, lean):
    order = jax.random.permutation(rng, number_of)
    crowded, usual = shares(number_of, rows * top, limit, lean, True), shares(number_of, rows * top, limit, lean, False)
    places = jnp.arange(number_of)

    def named(tallies, offset_by):
        used = int((tallies > 0).sum())
        fixed = max(1, used // 4)
        passed = fixed + (places - fixed + offset_by * (used - fixed)) % max(1, number_of - fixed)
        return jnp.zeros((number_of,), jnp.int32).at[order[jnp.where(places < fixed, places, passed)]].set(jnp.asarray(tallies, jnp.int32))

    tallies = jnp.where(number % 4 == 0, named(crowded, number // 4), named(usual, number - number // 4 - 1))
    mixed = jax.random.permutation(jax.random.fold_in(own, 3), number_of)
    donor, sink = mixed[0:number_of // 2 * 2:2], mixed[1:number_of // 2 * 2:2]
    margin = jnp.minimum(tallies[donor] - 1, limit - tallies[sink]) // 2
    margin = jnp.where((donor == order[0]) | (sink == order[0]) | (tallies[sink] == 0), 0, jnp.maximum(margin, 0))
    passed = jax.random.randint(jax.random.fold_in(own, 4), (number_of // 2,), 0, 1 << 20) % (margin + 1)
    tallies = tallies.at[donor].add(-passed).at[sink].add(passed)
    members = jnp.searchsorted(jnp.cumsum(tallies), jnp.arange(rows * top), side="right").astype(jnp.int32)
    table = members.reshape(top, rows).T
    table = table[jax.random.permutation(jax.random.fold_in(own, 1), rows)]
    offset_by = jax.random.randint(jax.random.fold_in(own, 2), (rows, 1), 0, top)
    return jnp.take_along_axis(table, (jnp.arange(top)[None, :] + offset_by) % top, axis=1)


def shares(count, total, bound, skew, full):
    weights = [(1 << 20) // math.isqrt(standing ** skew) + 1 for standing in range(1, count + 1)]
    largest = bound if full else min(bound, max(-(-total // count), total * weights[0] // sum(weights)))
    least = 1 if total - largest >= count - 1 else 0
    holding, rest = [largest] + [least] * (count - 1), total - largest - least * (count - 1)
    while rest > 0:
        movable = [i for i in range(1, count) if holding[i] < largest] or [i for i in range(1, count) if holding[i] < bound]
        whole, left = sum([weights[i] for i in movable]), rest
        for i in movable:
            addition = min(bound - holding[i], max(1, left * weights[i] // whole), rest)
            holding[i] = holding[i] + addition
            rest = rest - addition
    return np.array(holding)


def normal_values(key, extent, scale, most, shards=(), kind=jnp.bfloat16):
    loudness = steps_of(key, extent, shards, -0.22, 0.18) if shards else 1.0
    values = jax.random.normal(key, extent, jnp.float32) * scale * loudness
    return jnp.minimum(jnp.maximum(values, -most), most).astype(kind)


def setup_inputs(seed: int = 0) -> dict:
    keys = jax.random.split(jax.random.key(seed), 9)
    inputs = normal_values(keys[0], (SECTIONS, 2, TOKENS, D), 1.0, 6.0, ((0, 4), (2, 8)))
    routes_keys = jax.random.split(jax.random.fold_in(keys[1], 1), SECTIONS * 2 * TOKENS // TOK_DEV)
    routes_turns = jax.random.permutation(jax.random.fold_in(keys[1], 3), SECTIONS * 2 * TOKENS // TOK_DEV)
    routes = jax.vmap(lambda own, number: assign_block(jax.random.fold_in(keys[1], 2), own, number, TOK_DEV, EXPERTS, TOPK, CAP, 2))(routes_keys, routes_turns).reshape((SECTIONS, 2, TOKENS, TOPK))
    gates = jnp.clip(0.1 + 0.5 * jax.random.uniform(keys[2], (SECTIONS, 2, TOKENS, TOPK), jnp.float32) ** steps_of(keys[2], (SECTIONS, 2, TOKENS, TOPK), ((0, 4), (2, 8)), -0.2, 0.2), 0.1, 0.6)
    cot_early = normal_values(keys[3], (SECTIONS, TOKENS, D), 1.0, 6.0, ((0, 4), (1, 8)))
    head_grad = normal_values(keys[4], (TOKENS, D), 1.0, 6.0, ((0, 8),))
    w_gate = normal_values(keys[5], (SECTIONS, EXPERTS, D, FF_E), D ** -0.5, 0.125, ((0, 4), (1, 8)))
    w_up = normal_values(keys[6], (SECTIONS, EXPERTS, D, FF_E), D ** -0.5, 0.125, ((0, 4), (1, 8)))
    w_down = normal_values(keys[7], (SECTIONS, EXPERTS, FF_E, D), FF_E ** -0.5, 0.25, ((0, 4), (1, 8)))
    return {"inputs": inputs, "routes": routes, "gates": gates, "cot_early": cot_early, "head_grad": head_grad, "w_gate": w_gate, "w_up": w_up, "w_down": w_down}


def swish_parts(gate_value):
    sigmoid_value = jax.nn.sigmoid(gate_value)
    swished = gate_value * sigmoid_value
    derivative = sigmoid_value * (1.0 + gate_value * (1.0 - sigmoid_value))
    return swished, derivative


def expert_backward(row_inputs, row_grads, weight_gate, weight_up, weight_down, with_terms):
    gate_value = jnp.dot(row_inputs, weight_gate, preferred_element_type=jnp.float32)
    up_value = jnp.dot(row_inputs, weight_up, preferred_element_type=jnp.float32)
    swished, derivative = swish_parts(gate_value)
    grad_hidden = jnp.dot(row_grads, weight_down.T, preferred_element_type=jnp.float32)
    grad_gate_value = (grad_hidden * up_value * derivative).astype(jnp.bfloat16)
    grad_up_value = (grad_hidden * swished).astype(jnp.bfloat16)
    back_rows = (jnp.dot(grad_gate_value, weight_gate.T, preferred_element_type=jnp.float32)
                 + jnp.dot(grad_up_value, weight_up.T, preferred_element_type=jnp.float32)).astype(jnp.bfloat16)
    if not with_terms:
        return back_rows, ()
    hidden = (swished * up_value).astype(jnp.bfloat16)
    term_gate = jnp.dot(row_inputs.T, grad_gate_value, preferred_element_type=jnp.float32)
    term_up = jnp.dot(row_inputs.T, grad_up_value, preferred_element_type=jnp.float32)
    term_down = jnp.dot(hidden.T, row_grads, preferred_element_type=jnp.float32)
    return back_rows, (term_gate, term_up, term_down)


def layer_backward(tokens_in, route_ids, gate_weights, cotangent, weight_gate, weight_up, weight_down, with_terms):
    scaled = (gate_weights[:, :, None] * cotangent[:, None, :].astype(jnp.float32)).astype(jnp.bfloat16)
    scaled = scaled.reshape(TOKENS * TOPK, D)
    flat_ids = route_ids.reshape(-1)
    capacity = N_EXPERT * CAP

    def per_expert(summed, operands):
        expert_id, expert_gate, expert_up, expert_down = operands
        chosen = flat_ids == expert_id
        picked = jnp.argsort(jnp.where(chosen, 0, 1), stable=True)[:capacity].astype(jnp.int32)
        present = chosen[picked][:, None]
        row_inputs = jnp.where(present, tokens_in[picked // TOPK], jnp.zeros((), tokens_in.dtype))
        row_grads = jnp.where(present, scaled[picked], jnp.zeros((), scaled.dtype))
        back_rows, terms = expert_backward(row_inputs, row_grads, expert_gate, expert_up, expert_down, with_terms)
        summed = summed.at[picked].add(jnp.where(present, back_rows.astype(jnp.float32), jnp.zeros((), jnp.float32)))
        return summed, terms

    start = jnp.zeros((TOKENS * TOPK, D), jnp.float32)
    expert_ids = jnp.arange(EXPERTS, dtype=jnp.int32)
    summed, terms = lax.scan(per_expert, start, (expert_ids, weight_gate, weight_up, weight_down))
    result = cotangent.astype(jnp.float32) + jnp.sum(summed.reshape(TOKENS, TOPK, D), axis=1)
    return result.astype(jnp.bfloat16), terms


def reference(inputs, routes, gates, cot_early, head_grad, w_gate, w_up, w_down):
    def early_section(operands):
        tokens_in, route_ids, gate_weights, cotangent, weight_gate, weight_up, weight_down = operands
        result, unused = layer_backward(tokens_in[0], route_ids[0], gate_weights[0], cotangent,
                                        weight_gate, weight_up, weight_down, False)
        return result

    grad_early = lax.map(early_section, (inputs, routes, gates, cot_early, w_gate, w_up, w_down))
    cot_late = jnp.concatenate([grad_early[1:], head_grad[None]], axis=0)

    def late_section(operands):
        tokens_in, route_ids, gate_weights, first_cot, second_cot, weight_gate, weight_up, weight_down = operands
        unused, terms_first = layer_backward(tokens_in[0], route_ids[0], gate_weights[0], first_cot,
                                             weight_gate, weight_up, weight_down, True)
        result, terms_second = layer_backward(tokens_in[1], route_ids[1], gate_weights[1], second_cot,
                                              weight_gate, weight_up, weight_down, True)
        sums = tuple((terms_first[index] + terms_second[index]).astype(jnp.bfloat16) for index in range(3))
        return result, sums

    grad_late, sums = lax.map(late_section, (inputs, routes, gates, cot_early, cot_late, w_gate, w_up, w_down))
    return grad_early, grad_late, sums[0], sums[1], sums[2]
```

```python
import functools

import jax
import jax.numpy as jnp
from jax import lax
from jax.experimental import pallas as pl
from jax.experimental.pallas import tpu as pltpu
from jax.sharding import PartitionSpec as P

LANES = 128
VMEM_BYTES = 48 * 1024 * 1024
NT = (((1,), (1,)), ((), ()))
TN = (((0,), (0,)), ((), ()))
BF16 = jnp.bfloat16
F32 = jnp.float32


def dot(a, b, dims=(((1,), (0,)), ((), ()))):
    return lax.dot_general(a, b, dims, preferred_element_type=F32)


def params():
    return pltpu.CompilerParams(vmem_limit_bytes=VMEM_BYTES)


def cost(flops, moved):
    return pl.CostEstimate(flops=int(flops), bytes_accessed=int(moved), transcendentals=0)


class Grid:
    def __init__(self, count):
        self.ny = max(d for d in range(1, count + 1) if count % d == 0 and d * d <= count)
        self.nz = count // self.ny
        self.far = sorted(range(1, self.nz), key=lambda k: -min(k, self.nz - k))
        self.offsets = [(k, j) for k in [0] + self.far for j in range(self.ny)]

    def pairs(self, dz, dy):
        return [
            (z * self.ny + y, (z + dz) % self.nz * self.ny + (y + dy) % self.ny)
            for z in range(self.nz)
            for y in range(self.ny)
        ]

    def move(self, x, dz, dy):
        return lax.ppermute(x, "expert", self.pairs(dz, dy))

    def move_down(self, x, dz):
        sections, count = lax.axis_size("section"), lax.axis_size("expert")
        pairs = [
            (s * count + a, (s - 1) % sections * count + b)
            for s in range(sections)
            for a, b in self.pairs(dz, 0)
        ]
        return lax.ppermute(x, ("section", "expert"), pairs)

    def spread(self, along_z):
        found = {(k, 0): block for k, block in along_z.items()}
        for k in [0] + self.far:
            for j in range(1, self.ny):
                found[k, j] = self.move(along_z[k], 0, j)
        return [found[offset] for offset in self.offsets]

    def gather(self, x):
        along_z = {0: x}
        for k in self.far:
            along_z[k] = self.move(x, k, 0)
        return self.spread(along_z)

    def reduce(self, blocks):
        part = dict(zip(self.offsets, blocks))
        total = None
        for k in self.far + [0]:
            summed = part[k, 0].astype(F32)
            for j in range(1, self.ny):
                summed = summed + self.move(part[k, j], 0, -j).astype(F32)
            if k:
                summed = self.move(summed.astype(BF16), -k, 0).astype(F32)
            total = summed if total is None else total + summed
        return total


def join(refs, whole):
    rows = refs[0].shape[0]
    for i, ref in enumerate(refs):
        whole[i * rows : (i + 1) * rows, :] = ref[...]


def hidden_kernel(count, *refs):
    x_refs, (gate_w, up_w, x_out, gate_out, up_out) = refs[:count], refs[count:]

    @pl.when((pl.program_id(0) == 0) & (pl.program_id(1) == 0))
    def _():
        join(x_refs, x_out)

    x = x_out[...]
    gate_out[...] = dot(x, gate_w[0])
    up_out[...] = dot(x, up_w[0])


def hidden_values(blocks, w_gate, w_up):
    local, depth, width = w_gate.shape
    rows = blocks[0].shape[0]
    tokens = rows * len(blocks)
    tile = min(256, width)
    steps = width // tile
    whole = lambda e, f: (0, 0)
    at = lambda e, f: (0, e * steps + f)
    out = jax.ShapeDtypeStruct((tokens, local * width), F32)
    return pl.pallas_call(
        functools.partial(hidden_kernel, len(blocks)),
        grid=(local, steps),
        in_specs=[pl.BlockSpec((rows, depth), whole)] * len(blocks)
        + [pl.BlockSpec((1, depth, tile), lambda e, f: (e, 0, f))] * 2,
        out_specs=[
            pl.BlockSpec((tokens, depth), whole),
            pl.BlockSpec((tokens, tile), at),
            pl.BlockSpec((tokens, tile), at),
        ],
        out_shape=[jax.ShapeDtypeStruct((tokens, depth), BF16), out, out],
        compiler_params=params(),
        cost_estimate=cost(4 * tokens * depth * local * width, 4 * local * depth * width),
        name="hidden_values",
    )(*blocks, w_gate, w_up)


def grads_kernel(count, *refs):
    c_refs, g_refs = refs[:count], refs[count : 2 * count]
    pick, gate, up, down_w, c_out, grad_gate, grad_up, hidden, gates = refs[2 * count :]

    @pl.when((pl.program_id(0) == 0) & (pl.program_id(1) == 0))
    def _():
        join(c_refs, c_out)
        join(g_refs, gates)

    weight = dot(gates[...], pick[0])
    grad_hidden = dot(c_out[...], down_w[0], NT) * weight
    gate_value, up_value = gate[...], up[...]
    sigmoid_value = jax.nn.sigmoid(gate_value)
    swished = gate_value * sigmoid_value
    derivative = sigmoid_value * (1.0 + gate_value * (1.0 - sigmoid_value))
    hidden[...] = (swished * up_value * weight).astype(BF16)
    grad_gate[...] = (grad_hidden * up_value * derivative).astype(BF16)
    grad_up[...] = (grad_hidden * swished).astype(BF16)


def hidden_grads(blocks, gate_blocks, pick, gate, up, w_down):
    local, width, depth = w_down.shape
    rows = blocks[0].shape[0]
    tokens = rows * len(blocks)
    tile = pick.shape[-1]
    steps = width // tile
    whole = lambda e, f: (0, 0)
    at = lambda e, f: (0, e * steps + f)
    columns = gate_blocks[0].shape[1]
    out = jax.ShapeDtypeStruct((tokens, local * width), BF16)
    return pl.pallas_call(
        functools.partial(grads_kernel, len(blocks)),
        grid=(local, steps),
        in_specs=[pl.BlockSpec((rows, depth), whole)] * len(blocks)
        + [pl.BlockSpec((rows, columns), whole)] * len(blocks)
        + [
            pl.BlockSpec((1, columns, tile), lambda e, f: (e, 0, 0)),
            pl.BlockSpec((tokens, tile), at),
            pl.BlockSpec((tokens, tile), at),
            pl.BlockSpec((1, tile, depth), lambda e, f: (e, f, 0)),
        ],
        out_specs=[pl.BlockSpec((tokens, depth), whole)] + [pl.BlockSpec((tokens, tile), at)] * 3,
        out_shape=[jax.ShapeDtypeStruct((tokens, depth), BF16), out, out, out],
        scratch_shapes=[pltpu.VMEM((tokens, columns), BF16)],
        compiler_params=params(),
        cost_estimate=cost(2 * tokens * depth * local * width, 2 * local * depth * width),
        name="hidden_grads",
    )(*blocks, *gate_blocks, pick, gate, up, w_down)


def back_kernel(count, grad_gate, grad_up, gate_w, up_w, *outs):
    local, _, width = gate_w.shape
    total = None
    for e in range(local):
        columns = slice(e * width, (e + 1) * width)
        for grad, weight in ((grad_gate, gate_w), (grad_up, up_w)):
            term = dot(grad[:, columns], weight[e], NT)
            total = term if total is None else total + term
    total = total.astype(BF16)
    rows = outs[0].shape[0]
    for i in range(count):
        outs[i][...] = total[i * rows : (i + 1) * rows]


def back_rows(grad_gate, grad_up, w_gate, w_up, count):
    local, depth, width = w_gate.shape
    tokens = grad_gate.shape[0]
    rows = tokens // count
    tile = min(256, depth)
    whole = pl.BlockSpec(grad_gate.shape, lambda d: (0, 0))
    weight = pl.BlockSpec((local, tile, width), lambda d: (0, d, 0))
    return pl.pallas_call(
        functools.partial(back_kernel, count),
        grid=(depth // tile,),
        in_specs=[whole, whole, weight, weight],
        out_specs=[pl.BlockSpec((rows, tile), lambda d: (0, d))] * count,
        out_shape=[jax.ShapeDtypeStruct((rows, depth), BF16)] * count,
        compiler_params=params(),
        cost_estimate=cost(4 * tokens * depth * local * width, 4 * local * depth * width),
        name="back_rows",
    )(grad_gate, grad_up, w_gate, w_up)


def outer_kernel(lefts, rights, out):
    left = jnp.concatenate([ref[...] for ref in lefts], axis=0)
    right = jnp.concatenate([ref[...] for ref in rights], axis=0)
    out[0] = dot(left, right, TN).astype(BF16)


def outer_input_kernel(first_x, second_x, first, second, out):
    outer_kernel((first_x, second_x), (first, second), out)


def outer_input(first_x, second_x, first, second, local):
    tokens, depth = first_x.shape
    width = first.shape[1] // local
    tile = min(512, depth)
    x_spec = pl.BlockSpec((tokens, tile), lambda e, d: (0, d))
    g_spec = pl.BlockSpec((tokens, width), lambda e, d: (0, e))
    return pl.pallas_call(
        outer_input_kernel,
        grid=(local, depth // tile),
        in_specs=[x_spec, x_spec, g_spec, g_spec],
        out_specs=pl.BlockSpec((1, tile, width), lambda e, d: (e, d, 0)),
        out_shape=jax.ShapeDtypeStruct((local, depth, width), BF16),
        compiler_params=params(),
        cost_estimate=cost(4 * tokens * depth * local * width, 2 * local * depth * width),
        name="outer_input",
    )(first_x, second_x, first, second)


def outer_hidden(first_hidden, second_hidden, first_c, second_c, local):
    tokens, depth = first_c.shape
    width = first_hidden.shape[1] // local
    tile = min(256, width)
    steps = width // tile
    h_spec = pl.BlockSpec((tokens, tile), lambda e, f: (0, e * steps + f))
    c_spec = pl.BlockSpec((tokens, depth), lambda e, f: (0, 0))
    return pl.pallas_call(
        outer_input_kernel,
        grid=(local, steps),
        in_specs=[h_spec, h_spec, c_spec, c_spec],
        out_specs=pl.BlockSpec((1, tile, depth), lambda e, f: (e, f, 0)),
        out_shape=jax.ShapeDtypeStruct((local, width, depth), BF16),
        compiler_params=params(),
        cost_estimate=cost(4 * tokens * depth * local * width, 2 * local * depth * width),
        name="outer_hidden",
    )(first_hidden, second_hidden, first_c, second_c)


def gate_columns(routes, gates, experts):
    chosen = routes[:, :, None] == jnp.arange(experts, dtype=jnp.int32)[None, None, :]
    dense = jnp.sum(jnp.where(chosen, gates[:, :, None], 0.0), axis=1)
    high = lax.reduce_precision(dense, 8, 7)
    middle = lax.reduce_precision(dense - high, 8, 7)
    low = dense - high - middle
    columns = jnp.concatenate([high, middle, low], axis=1).astype(BF16)
    return jnp.pad(columns, ((0, 0), (0, -columns.shape[1] % LANES)))


def on_device(inputs, routes, gates, cot_early, head_grad, w_gate, w_up, w_down):
    w_gate, w_up, w_down = w_gate[0], w_up[0], w_down[0]
    grid = Grid(lax.axis_size("expert"))
    me = lax.axis_index("expert")
    local, depth, width = w_gate.shape
    experts = local * lax.axis_size("expert")
    first_in, second_in = inputs[0, 0], inputs[0, 1]
    first_cot = cot_early[0]
    first_g = gate_columns(routes[0, 0], gates[0, 0], experts)
    second_g = gate_columns(routes[0, 1], gates[0, 1], experts)
    columns = first_g.shape[1]
    own = me * local + jnp.arange(local, dtype=jnp.int32)
    lane = jnp.arange(columns, dtype=jnp.int32)
    mine = (lane[None, :] % experts == own[:, None]) & (lane[None, :] < 3 * experts)
    pick = jnp.broadcast_to(
        mine[:, :, None], (local, columns, min(256, width))
    ).astype(BF16)

    first_blocks = grid.gather(first_in)
    first_x, first_gate, first_up = hidden_values(first_blocks, w_gate, w_up)
    joined = grid.gather(jnp.concatenate([first_cot, first_g], axis=1))
    first_c, first_dg, first_du, first_h = hidden_grads(
        [b[:, :depth] for b in joined],
        [b[:, depth:] for b in joined],
        pick, first_gate, first_up, w_down,
    )
    first_back = back_rows(first_dg, first_du, w_gate, w_up, len(joined))
    grad_early = (first_cot.astype(F32) + grid.reduce(first_back)).astype(BF16)

    sent = jnp.where(lax.axis_index("section") == 0, head_grad, grad_early)
    joined = grid.gather(jnp.concatenate([second_in, second_g], axis=1))
    second_x, second_gate, second_up = hidden_values(
        [b[:, :depth] for b in joined], w_gate, w_up
    )
    along_z = {k: grid.move_down(sent, k) for k in grid.far + [0]}
    second_cot = along_z[0]
    second_c, second_dg, second_du, second_h = hidden_grads(
        grid.spread(along_z),
        [b[:, depth:] for b in joined],
        pick, second_gate, second_up, w_down,
    )
    second_back = back_rows(second_dg, second_du, w_gate, w_up, len(joined))
    grad_late = (second_cot.astype(F32) + grid.reduce(second_back)).astype(BF16)
    grad_gate = outer_input(first_x, second_x, first_dg, second_dg, local)
    grad_up = outer_input(first_x, second_x, first_du, second_du, local)
    grad_down = outer_hidden(first_h, second_h, first_c, second_c, local)
    return (grad_early[None], grad_late[None], grad_gate[None], grad_up[None], grad_down[None])


def solution(mesh):
    in_specs = (
        P("section", None, "expert", None),
        P("section", None, "expert", None),
        P("section", None, "expert", None),
        P("section", "expert", None),
        P("expert", None),
        P("section", "expert", None, None),
        P("section", "expert", None, None),
        P("section", "expert", None, None),
    )
    out_specs = (
        P("section", "expert", None),
        P("section", "expert", None),
        P("section", "expert", None, None),
        P("section", "expert", None, None),
        P("section", "expert", None, None),
    )
    return jax.shard_map(
        on_device, mesh=mesh, in_specs=in_specs, out_specs=out_specs, check_vma=False
    )
```

```python
import functools

import jax
import jax.numpy as jnp
from jax import lax
from jax.experimental import pallas as pl
from jax.experimental.pallas import tpu as pltpu
from jax.sharding import PartitionSpec as P

LANES = 128
VMEM_BYTES = 60 * 1024 * 1024
OUTER_VMEM_BYTES = 20 * 1024 * 1024
NT = (((1,), (1,)), ((), ()))
TN = (((0,), (0,)), ((), ()))
BF16 = jnp.bfloat16
F32 = jnp.float32


def dot(a, b, dims=(((1,), (0,)), ((), ()))):
    return lax.dot_general(a, b, dims, preferred_element_type=F32)


class Grid:
    def __init__(self, count):
        self.ny = max(d for d in range(1, count + 1) if count % d == 0 and d * d <= count)
        self.nz = count // self.ny
        self.far = sorted(range(1, self.nz), key=lambda k: (min(k, self.nz - k), -k))
        self.along = [0] + self.far

    def pairs(self, dz, dy):
        return [
            (z * self.ny + y, (z + dz) % self.nz * self.ny + (y + dy) % self.ny)
            for z in range(self.nz)
            for y in range(self.ny)
        ]

    def move(self, x, dz, dy):
        with jax.named_scope(f"z{dz}y{dy}"):
            return lax.ppermute(x, "expert", self.pairs(dz, dy))

    def move_down(self, x, dz):
        sections, count = lax.axis_size("section"), lax.axis_size("expert")
        pairs = [
            (s * count + a, (s - 1) % sections * count + b)
            for s in range(sections)
            for a, b in self.pairs(dz, 0)
        ]
        with jax.named_scope(f"down_z{dz}"):
            return lax.ppermute(x, ("section", "expert"), pairs)

    def along_z(self, x):
        return [x] + [self.move(x, k, 0) for k in self.far]

    def near(self, x):
        return [self.move(x, 0, j) for j in range(1, self.ny)]

    def reduce_y(self, parts):
        move = lambda *x: [self.move(part, 0, -j) for j, part in enumerate(x, 1)]
        summed = parts[0].astype(F32)
        for moved in move(*parts[1:]):
            summed = summed + moved.astype(F32)
        rows = summed.shape[0] // self.nz
        own = summed[:rows]
        return own, [summed[i * rows : (i + 1) * rows].astype(BF16) for i in range(1, self.nz)]

    def reduce_z(self, own, blocks, turn):
        move = lambda *x: [self.move(block, -k, 0) for k, block in zip(self.far, x)]
        for moved in turn("z", move, *blocks):
            own = own + moved.astype(F32)
        return own


def on_core(kernel, name, flops, index, operands, out_shape, scratch):
    hbm = pl.BlockSpec(memory_space=pltpu.HBM)
    return pl.pallas_call(
        kernel,
        in_specs=[pl.BlockSpec(memory_space=pltpu.SMEM)] * len(index) + [hbm] * len(operands),
        out_specs=[hbm] * len(out_shape),
        out_shape=out_shape,
        scratch_shapes=scratch,
        compiler_params=pltpu.CompilerParams(vmem_limit_bytes=VMEM_BYTES),
        cost_estimate=pl.CostEstimate(flops=int(flops), bytes_accessed=0, transcendentals=0),
        name=name,
    )(*index, *operands)


def join(refs, whole, place, sem):
    rows, block, at = place
    copies, start = [], 0
    for ref in refs:
        for first in range(at[0], ref.shape[0], block):
            copies.append(
                pltpu.make_async_copy(
                    ref.at[first : first + rows, at[1] : at[1] + whole.shape[1]],
                    whole.at[start : start + rows, :],
                    sem.at[len(copies)],
                )
            )
            start += rows
    return copies


def tiles(size):
    tile = min(256, size)
    return [slice(i, i + tile) for i in range(0, size, tile)]


def rows_kernel(counts, places, lane, count, me, *refs):
    refs = list(refs)
    take = lambda n: [refs.pop(0) for _ in range(n)]
    x_refs, c_refs, g_refs = (take(n) for n in counts)
    weights_hbm = take(3)
    x_hbm, c_hbm = take(2)
    values_hbm, outs = take(3), take(count)
    weights, values = take(3), take(3)
    x, c, g, gate, up, back, total_out, x_sem, c_sem, g_sem, w_sem, v_sem, out_sem = refs
    gate_w, up_w, down_w = weights
    grad_gate, grad_up, hidden = values
    local, depth, width = gate_w.shape
    rows = outs[0].shape[0]
    x_copies = join(x_refs, x, places[0], x_sem)
    c_copies = join(c_refs, c, places[1], c_sem)
    g_copies = join(g_refs, g, places[2], g_sem)
    queue = [
        pltpu.make_async_copy(weights_hbm[i].at[e], weights[i].at[e], w_sem.at[i * local + e])
        for e in range(local)
        for i in (2, 0, 1)
    ]

    def arrived(position):
        if position + 2 < len(queue):
            queue[position + 2].start()
        queue[position].wait()

    for copy in c_copies + g_copies + queue[:1] + x_copies + queue[1:2]:
        copy.start()
    for copy in c_copies + g_copies:
        copy.wait()
    writes = []

    def write(*copy):
        writes.append(pltpu.make_async_copy(*copy))
        writes[-1].start()

    experts = lane[1]
    at_lane = lax.broadcasted_iota(jnp.int32, (g.shape[1], tiles(width)[0].stop), 0)
    for e in range(local):
        arrived(3 * e)
        first = lane[0] + me[0] * local + e
        mine = (at_lane == first) | (at_lane == first + experts) | (at_lane == first + 2 * experts)
        weight = dot(g[...], mine.astype(F32).astype(BF16))
        grads = [dot(c[...], down_w[e, f, :], NT) * weight for f in tiles(width)]
        if e == 0:
            for copy in x_copies:
                copy.wait()
        arrived(3 * e + 1)
        if e == local - 1:
            write(x, x_hbm, v_sem.at[3])
            write(c, c_hbm, v_sem.at[4])
        for f in tiles(width):
            gate[:, f] = dot(x[...], gate_w[e, :, f])
        arrived(3 * e + 2)
        for f in tiles(width):
            up[:, f] = dot(x[...], up_w[e, :, f])
        for f, grad_hidden in zip(tiles(width), grads):
            at = slice(e * width + f.start, e * width + f.stop)
            gate_value, up_value = gate[:, f], up[:, f]
            sigmoid_value = jax.nn.sigmoid(gate_value)
            swished = gate_value * sigmoid_value
            derivative = sigmoid_value * (1.0 + gate_value * (1.0 - sigmoid_value))
            hidden[:, at] = (swished * up_value * weight).astype(BF16)
            grad_gate[:, at] = (grad_hidden * up_value * derivative).astype(BF16)
            grad_up[:, at] = (grad_hidden * swished).astype(BF16)
        columns = slice(e * width, (e + 1) * width)
        if e == local - 1:
            for i in range(3):
                write(values[i], values_hbm[i], v_sem.at[i])
        for d in tiles(depth):
            total = dot(grad_gate[:, columns], gate_w[e, d, :], NT)
            total = total + dot(grad_up[:, columns], up_w[e, d, :], NT)
            if e:
                total = total + back[:, d]
            if e < local - 1:
                back[:, d] = total
                continue
            total_out[:, d] = total.astype(BF16)
            if d.stop in (depth // 2, depth):
                side = slice(d.stop - depth // 2, d.stop)
                for j, out in enumerate(outs):
                    sem = out_sem.at[j, d.stop // depth]
                    write(total_out.at[j * rows : (j + 1) * rows, side], out.at[:, side], sem)
    for copy in writes:
        copy.wait()


def expert_rows(tokens, blocks, places, lane, lanes, me, weights, count):
    local, depth, width = weights[0].shape
    value = (tokens, local * width)
    return on_core(
        functools.partial(rows_kernel, [len(x) for x in blocks], places, lane, count),
        "expert_rows",
        10 * tokens * depth * local * width,
        [me],
        [*blocks[0], *blocks[1], *blocks[2], *weights],
        [jax.ShapeDtypeStruct((tokens, depth), BF16)] * 2
        + [jax.ShapeDtypeStruct(value, BF16)] * 3
        + [jax.ShapeDtypeStruct((tokens // count, depth), BF16)] * count,
        [pltpu.VMEM(w.shape, BF16) for w in weights]
        + [pltpu.VMEM(value, BF16)] * 3
        + [pltpu.VMEM((tokens, depth), BF16)] * 2
        + [pltpu.VMEM((tokens, lanes), BF16)]
        + [pltpu.VMEM((tokens, width), F32)] * 2
        + [pltpu.VMEM((tokens, depth), F32), pltpu.VMEM((tokens, depth), BF16)]
        + [pltpu.SemaphoreType.DMA((tokens // place[0],)) for place in places]
        + [pltpu.SemaphoreType.DMA((3 * local,)), pltpu.SemaphoreType.DMA((5,))]
        + [pltpu.SemaphoreType.DMA((count, 2))],
    )


def outer_kernel(pieces, *refs):
    lefts, rights = refs[:pieces], refs[pieces : 2 * pieces]
    out, right = refs[2 * pieces :]
    local, rows, columns = out.shape
    start = 0
    for ref in rights:
        right[start : start + ref.shape[0], :] = ref[...]
        start += ref.shape[0]
    for m in tiles(lefts[0].shape[1]):
        left = jnp.concatenate([ref[:, m] for ref in lefts], axis=0)
        product = dot(left, right[...], TN).astype(BF16)
        if lefts[0].shape[1] == rows:
            for e in range(local):
                out[e, m, :] = product[:, e * columns : (e + 1) * columns]
        else:
            at = m.start % rows
            out[m.start // rows, at : at + m.stop - m.start, :] = product


def outer(lefts, rights, local, rows, columns, name):
    tokens = sum(x.shape[0] for x in lefts)
    spec = pl.BlockSpec(memory_space=pltpu.VMEM)
    return pl.pallas_call(
        functools.partial(outer_kernel, len(lefts)),
        in_specs=[spec] * (2 * len(lefts)),
        out_specs=spec,
        out_shape=jax.ShapeDtypeStruct((local, rows, columns), BF16),
        scratch_shapes=[pltpu.VMEM((tokens, rights[0].shape[1]), BF16)],
        compiler_params=pltpu.CompilerParams(vmem_limit_bytes=OUTER_VMEM_BYTES),
        cost_estimate=pl.CostEstimate(
            flops=2 * tokens * local * rows * columns, bytes_accessed=0, transcendentals=0
        ),
        name=name,
    )(*lefts, *rights)


def payload_kernel(experts, half, routes, gates, x_in, c_in, *refs):
    *outs, columns, sems = refs
    rows, depth = half, x_in.shape[-1]
    copies = []
    for i, out in enumerate(outs):
        from_rows = slice(i * rows, (i + 1) * rows)
        for j, source in enumerate((x_in.at[0, 0], c_in.at[0])):
            copies.append(
                pltpu.make_async_copy(
                    source.at[from_rows, :],
                    out.at[:, j * depth : (j + 1) * depth],
                    sems.at[len(copies)],
                )
            )
    for copy in copies:
        copy.start()
    lanes = columns.shape[1]
    lane = lax.broadcasted_iota(jnp.int32, (lanes, rows), 0)
    group = lane // (3 * experts)
    part = lane // experts % 3
    expert = lane % experts
    dense = jnp.zeros((lanes, rows), F32)
    for m in range(routes.shape[2]):
        for i in range(len(outs)):
            here = group == m * len(outs) + i
            chosen = routes[0, :, m, i * rows : (i + 1) * rows]
            weight = gates[0, :, m, i * rows : (i + 1) * rows]
            for k in range(chosen.shape[0]):
                named = here & (chosen[k : k + 1, :] == expert)
                dense = dense + jnp.where(named, weight[k : k + 1, :], 0.0)
    high = dense.astype(BF16)
    rest = dense - high.astype(F32)
    middle = rest.astype(BF16)
    low = (rest - middle.astype(F32)).astype(BF16)
    pieces = [x.astype(F32) for x in (high, middle, low)]
    chosen = jnp.where(part == 0, pieces[0], jnp.where(part == 1, pieces[1], pieces[2]))
    columns[...] = jnp.transpose(chosen).astype(BF16)
    outs[0][:, 2 * depth :] = columns[...]
    for copy in copies:
        copy.wait()


def payloads(routes, gates, inputs, cot_early, experts):
    half, depth = inputs.shape[2] // 2, inputs.shape[3]
    lanes = 2 * 2 * 3 * experts
    lanes += -lanes % LANES
    small = pl.BlockSpec(memory_space=pltpu.VMEM)
    large = pl.BlockSpec(memory_space=pltpu.HBM)
    return pl.pallas_call(
        functools.partial(payload_kernel, experts, half),
        in_specs=[small, small, large, large],
        out_specs=[small, small],
        out_shape=[
            jax.ShapeDtypeStruct((half, 2 * depth + lanes), BF16),
            jax.ShapeDtypeStruct((half, 2 * depth), BF16),
        ],
        scratch_shapes=[pltpu.VMEM((half, lanes), BF16), pltpu.SemaphoreType.DMA((4,))],
        compiler_params=pltpu.CompilerParams(vmem_limit_bytes=VMEM_BYTES),
        name="payloads",
    )(jnp.moveaxis(routes, 3, 1), jnp.moveaxis(gates, 3, 1), inputs, cot_early)


def after(x, *done):
    return lax.optimization_barrier((x, done))[0]


def on_device(inputs, routes, gates, cot_early, head_grad, w_gate, w_up, w_down):
    w_gate, w_up, w_down = w_gate[0], w_up[0], w_down[0]
    grid = Grid(lax.axis_size("expert"))
    me = lax.axis_index("expert")
    local, depth, width = w_gate.shape
    experts = local * lax.axis_size("expert")
    first_in, second_in = inputs[0, 0], inputs[0, 1]
    first_cot = cot_early[0]
    tokens = first_in.shape[0]
    half = tokens // 2
    halves = [slice(0, half), slice(half, tokens)]
    is_first = lax.axis_index("section") == 0
    everyone = half * grid.nz * grid.ny
    a0, b0 = payloads(routes, gates, inputs, cot_early, experts)
    lanes = a0.shape[1] - 2 * depth
    me = jnp.full((1,), lax.axis_index("expert"), jnp.int32)
    weights = (w_gate, w_up, w_down)

    def fuse(blocks):
        return jnp.concatenate(blocks, axis=0)

    def mix(*values):
        return [part for group in zip(*values) for part in group]

    def rows_of(m, part, x, c):
        results = expert_rows(
            everyone, (x[0], c[0], gate_blocks), (x[1], c[1], (half, half, (0, 2 * depth))),
            ((2 * m + part) * 3 * experts, experts), lanes, me, weights, grid.ny,
        )
        for kept, value in zip((xs, cs, dgs, dus, hs), results):
            kept.append(value)
        return results[5:]

    xs, cs, dgs, dus, hs = [], [], [], [], []

    def early_rows(part, blocks):
        return rows_of(0, part, (blocks, (half, half, (0, 0))), (blocks, (half, half, (0, depth))))

    def late_rows(part, blocks):
        x = (second_blocks, (half, tokens, (halves[part].start, 0)))
        return rows_of(1, part, x, (blocks, (half, half, (0, 0))))

    def early_grad(part, total):
        rows = halves[part]
        grad = (first_cot[rows].astype(F32) + total).astype(BF16)
        return grad, jnp.where(is_first, head_grad[rows], grad)

    last = {"z": (), "y": ()}

    def turn(link, move, *x):
        x = after(x, last[link])
        last[link] = move(*x)
        return last[link]

    straight = lambda link, move, *x: move(*x)
    a, b = halves
    along_z = lambda x: grid.along_z(x)[1:]
    ya, yb, yx = grid.near(a0), grid.near(b0), grid.near(second_in)
    za = turn("z", along_z, a0)
    fa = grid.near(after(fuse(za), ya, yb, yx))
    zb = turn("z", along_z, b0)
    gate_blocks = [a0] + za + mix(ya, fa)
    fb = grid.near(fuse(zb))
    zx = turn("z", along_z, second_in)
    back_a = early_rows(0, gate_blocks)
    own_a, sums_a = grid.reduce_y(back_a)
    back_b = early_rows(1, after([b0] + zb + mix(yb, fb), zx))
    total_a = grid.reduce_z(own_a, sums_a, turn)
    own_b, sums_b = grid.reduce_y(back_b)
    early_a, sent_a = early_grad(0, total_a)
    move_down = lambda *x: [grid.move_down(x[0], k) for k in grid.along]
    down_a = turn("z", move_down, sent_a)
    fx = grid.near(fuse(zx))
    second_blocks = [second_in] + zx + mix(yx, fx)
    total_b = grid.reduce_z(own_b, sums_b, straight)
    fa = grid.near(fuse(down_a))
    early_b, sent_b = early_grad(1, total_b)
    down_b = turn("z", move_down, sent_b)
    late_back_a = late_rows(0, down_a + fa)
    fb = grid.near(fuse(down_b))
    own_a, sums_a = grid.reduce_y(late_back_a)
    late_back_b = late_rows(1, down_b + fb)
    total_a = grid.reduce_z(own_a, sums_a, turn)
    own_b, sums_b = grid.reduce_y(late_back_b)
    total_b = grid.reduce_z(own_b, sums_b, turn)
    grad_late_a = (down_a[0].astype(F32) + total_a).astype(BF16)
    grad_late_b = (down_b[0].astype(F32) + total_b).astype(BF16)
    grad_gate = outer(after(xs, late_back_b, sums_a), dgs, local, depth, width, "outer_gate")
    grad_up = outer(after(xs, sums_b), dus, local, depth, width, "outer_up")
    grad_down = outer(after(hs, sums_b), cs, local, width, depth, "outer_down")
    grad_early = jnp.concatenate([early_a, early_b], axis=0)
    grad_late = jnp.concatenate([grad_late_a, grad_late_b], axis=0)
    return (grad_early[None], grad_late[None], grad_gate[None], grad_up[None], grad_down[None])


def solution(mesh):
    in_specs = (
        P("section", None, "expert", None),
        P("section", None, "expert", None),
        P("section", None, "expert", None),
        P("section", "expert", None),
        P("expert", None),
        P("section", "expert", None, None),
        P("section", "expert", None, None),
        P("section", "expert", None, None),
    )
    out_specs = (
        P("section", "expert", None),
        P("section", "expert", None),
        P("section", "expert", None, None),
        P("section", "expert", None, None),
        P("section", "expert", None, None),
    )
    return jax.shard_map(
        on_device, mesh=mesh, in_specs=in_specs, out_specs=out_specs, check_vma=False
    )
```

```python
import functools

import jax
import jax.numpy as jnp
from jax import lax
from jax.experimental import pallas as pl
from jax.experimental.pallas import tpu as pltpu
from jax.sharding import PartitionSpec as P

LANES = 128
VMEM_BYTES = 60 * 1024 * 1024
OUTER_VMEM_BYTES = 20 * 1024 * 1024
NT = (((1,), (1,)), ((), ()))
TN = (((0,), (0,)), ((), ()))
BF16 = jnp.bfloat16
F32 = jnp.float32


def dot(a, b, dims=(((1,), (0,)), ((), ()))):
    return lax.dot_general(a, b, dims, preferred_element_type=F32)


class Grid:
    def __init__(self, count):
        self.ny = max(d for d in range(1, count + 1) if count % d == 0 and d * d <= count)
        self.nz = count // self.ny
        self.far = sorted(range(1, self.nz), key=lambda k: (min(k, self.nz - k), -k))
        self.along = [0] + self.far

    def pairs(self, dz, dy):
        return [
            (z * self.ny + y, (z + dz) % self.nz * self.ny + (y + dy) % self.ny)
            for z in range(self.nz)
            for y in range(self.ny)
        ]

    def move(self, x, dz, dy):
        with jax.named_scope(f"z{dz}y{dy}"):
            return lax.ppermute(x, "expert", self.pairs(dz, dy))

    def move_down(self, x, dz):
        sections, count = lax.axis_size("section"), lax.axis_size("expert")
        pairs = [
            (s * count + a, (s - 1) % sections * count + b)
            for s in range(sections)
            for a, b in self.pairs(dz, 0)
        ]
        with jax.named_scope(f"down_z{dz}"):
            return lax.ppermute(x, ("section", "expert"), pairs)

    def along_z(self, x):
        return [x] + [self.move(x, k, 0) for k in self.far]

    def near(self, x):
        return [self.move(x, 0, j) for j in range(1, self.ny)]

    def reduce_y(self, parts):
        move = lambda *x: [self.move(part, 0, -j) for j, part in enumerate(x, 1)]
        summed = parts[0].astype(F32)
        for moved in move(*parts[1:]):
            summed = summed + moved.astype(F32)
        rows = summed.shape[0] // self.nz
        own = summed[:rows]
        return own, [summed[i * rows : (i + 1) * rows].astype(BF16) for i in range(1, self.nz)]

    def reduce_z(self, own, blocks, turn):
        move = lambda *x: [self.move(block, -k, 0) for k, block in zip(self.far, x)]
        for moved in turn("z", move, *blocks):
            own = own + moved.astype(F32)
        return own


def on_core(kernel, name, flops, index, operands, out_shape, scratch):
    hbm = pl.BlockSpec(memory_space=pltpu.HBM)
    return pl.pallas_call(
        kernel,
        in_specs=[pl.BlockSpec(memory_space=pltpu.SMEM)] * len(index) + [hbm] * len(operands),
        out_specs=[hbm] * len(out_shape),
        out_shape=out_shape,
        scratch_shapes=scratch,
        compiler_params=pltpu.CompilerParams(vmem_limit_bytes=VMEM_BYTES),
        cost_estimate=pl.CostEstimate(flops=int(flops), bytes_accessed=0, transcendentals=0),
        name=name,
    )(*index, *operands)


def join(refs, whole, place, sem):
    rows, block, at = place
    copies, start = [], 0
    for ref in refs:
        for first in range(at[0], ref.shape[0], block):
            copies.append(
                pltpu.make_async_copy(
                    ref.at[first : first + rows, at[1] : at[1] + whole.shape[1]],
                    whole.at[start : start + rows, :],
                    sem.at[len(copies)],
                )
            )
            start += rows
    return copies


def tiles(size):
    tile = min(256, size)
    return [slice(i, i + tile) for i in range(0, size, tile)]


def rows_kernel(counts, places, lane, count, me, *refs):
    refs = list(refs)
    take = lambda n: [refs.pop(0) for _ in range(n)]
    x_refs, c_refs, g_refs = (take(n) for n in counts)
    weights_hbm = take(3)
    x_hbm, c_hbm = take(2)
    values_hbm, outs = take(3), take(count)
    weights, values = take(3), take(3)
    x, c, g, gate, up, back, total_out, x_sem, c_sem, g_sem, w_sem, v_sem, out_sem = refs
    gate_w, up_w, down_w = weights
    grad_gate, grad_up, hidden = values
    local, depth, width = gate_w.shape
    rows = outs[0].shape[0]
    x_copies = join(x_refs, x, places[0], x_sem)
    c_copies = join(c_refs, c, places[1], c_sem)
    g_copies = join(g_refs, g, places[2], g_sem)
    queue = [
        pltpu.make_async_copy(weights_hbm[i].at[e], weights[i].at[e], w_sem.at[i * local + e])
        for e in range(local)
        for i in (2, 0, 1)
    ]

    def arrived(position):
        if position + 2 < len(queue):
            queue[position + 2].start()
        queue[position].wait()

    for copy in c_copies + g_copies + queue[:1] + x_copies + queue[1:2]:
        copy.start()
    for copy in c_copies + g_copies:
        copy.wait()
    writes = []

    def write(*copy):
        writes.append(pltpu.make_async_copy(*copy))
        writes[-1].start()

    experts = lane[1]
    at_lane = lax.broadcasted_iota(jnp.int32, (g.shape[1], tiles(width)[0].stop), 0)
    for e in range(local):
        arrived(3 * e)
        first = lane[0] + me[0] * local + e
        mine = (at_lane == first) | (at_lane == first + experts) | (at_lane == first + 2 * experts)
        weight = dot(g[...], mine.astype(F32).astype(BF16))
        grads = [dot(c[...], down_w[e, f, :], NT) * weight for f in tiles(width)]
        if e == 0:
            for copy in x_copies:
                copy.wait()
        arrived(3 * e + 1)
        if e == local - 1:
            write(x, x_hbm, v_sem.at[3])
            write(c, c_hbm, v_sem.at[4])
        for f in tiles(width):
            gate[:, f] = dot(x[...], gate_w[e, :, f])
        arrived(3 * e + 2)
        for f in tiles(width):
            up[:, f] = dot(x[...], up_w[e, :, f])
        for f, grad_hidden in zip(tiles(width), grads):
            at = slice(e * width + f.start, e * width + f.stop)
            gate_value, up_value = gate[:, f], up[:, f]
            sigmoid_value = jax.nn.sigmoid(gate_value)
            swished = gate_value * sigmoid_value
            derivative = sigmoid_value * (1.0 + gate_value * (1.0 - sigmoid_value))
            hidden[:, at] = (swished * up_value * weight).astype(BF16)
            grad_gate[:, at] = (grad_hidden * up_value * derivative).astype(BF16)
            grad_up[:, at] = (grad_hidden * swished).astype(BF16)
        columns = slice(e * width, (e + 1) * width)
        if e == local - 1:
            for i in range(3):
                write(values[i], values_hbm[i], v_sem.at[i])
        for d in tiles(depth):
            total = dot(grad_gate[:, columns], gate_w[e, d, :], NT)
            total = total + dot(grad_up[:, columns], up_w[e, d, :], NT)
            if e:
                total = total + back[:, d]
            if e < local - 1:
                back[:, d] = total
                continue
            total_out[:, d] = total.astype(BF16)
            if d.stop in (depth // 2, depth):
                side = slice(d.stop - depth // 2, d.stop)
                for j, out in enumerate(outs):
                    sem = out_sem.at[j, d.stop // depth]
                    write(total_out.at[j * rows : (j + 1) * rows, side], out.at[:, side], sem)
    for copy in writes:
        copy.wait()


def expert_rows(tokens, blocks, places, lane, lanes, me, weights, count):
    local, depth, width = weights[0].shape
    value = (tokens, local * width)
    return on_core(
        functools.partial(rows_kernel, [len(x) for x in blocks], places, lane, count),
        "expert_rows",
        10 * tokens * depth * local * width,
        [me],
        [*blocks[0], *blocks[1], *blocks[2], *weights],
        [jax.ShapeDtypeStruct((tokens, depth), BF16)] * 2
        + [jax.ShapeDtypeStruct(value, BF16)] * 3
        + [jax.ShapeDtypeStruct((tokens // count, depth), BF16)] * count,
        [pltpu.VMEM(w.shape, BF16) for w in weights]
        + [pltpu.VMEM(value, BF16)] * 3
        + [pltpu.VMEM((tokens, depth), BF16)] * 2
        + [pltpu.VMEM((tokens, lanes), BF16)]
        + [pltpu.VMEM((tokens, width), F32)] * 2
        + [pltpu.VMEM((tokens, depth), F32), pltpu.VMEM((tokens, depth), BF16)]
        + [pltpu.SemaphoreType.DMA((tokens // place[0],)) for place in places]
        + [pltpu.SemaphoreType.DMA((3 * local,)), pltpu.SemaphoreType.DMA((5,))]
        + [pltpu.SemaphoreType.DMA((count, 2))],
    )


def outer_kernel(pieces, *refs):
    lefts, rights = refs[:pieces], refs[pieces : 2 * pieces]
    out, right = refs[2 * pieces :]
    local, rows, columns = out.shape
    start = 0
    for ref in rights:
        right[start : start + ref.shape[0], :] = ref[...]
        start += ref.shape[0]
    for m in tiles(lefts[0].shape[1]):
        left = jnp.concatenate([ref[:, m] for ref in lefts], axis=0)
        product = dot(left, right[...], TN).astype(BF16)
        if lefts[0].shape[1] == rows:
            for e in range(local):
                out[e, m, :] = product[:, e * columns : (e + 1) * columns]
        else:
            at = m.start % rows
            out[m.start // rows, at : at + m.stop - m.start, :] = product


def outer(lefts, rights, local, rows, columns, name):
    tokens = sum(x.shape[0] for x in lefts)
    spec = pl.BlockSpec(memory_space=pltpu.VMEM)
    return pl.pallas_call(
        functools.partial(outer_kernel, len(lefts)),
        in_specs=[spec] * (2 * len(lefts)),
        out_specs=spec,
        out_shape=jax.ShapeDtypeStruct((local, rows, columns), BF16),
        scratch_shapes=[pltpu.VMEM((tokens, rights[0].shape[1]), BF16)],
        compiler_params=pltpu.CompilerParams(vmem_limit_bytes=OUTER_VMEM_BYTES),
        cost_estimate=pl.CostEstimate(
            flops=2 * tokens * local * rows * columns, bytes_accessed=0, transcendentals=0
        ),
        name=name,
    )(*lefts, *rights)


def payload_kernel(experts, half, routes, gates, x_in, c_in, *refs):
    *outs, columns, sems = refs
    rows, depth = half, x_in.shape[-1]
    copies = []
    for i, out in enumerate(outs):
        from_rows = slice(i * rows, (i + 1) * rows)
        for j, source in enumerate((x_in.at[0, 0], c_in.at[0])):
            copies.append(
                pltpu.make_async_copy(
                    source.at[from_rows, :],
                    out.at[:, j * depth : (j + 1) * depth],
                    sems.at[len(copies)],
                )
            )
    for copy in copies:
        copy.start()
    lanes = columns.shape[1]
    lane = lax.broadcasted_iota(jnp.int32, (lanes, rows), 0)
    group = lane // (3 * experts)
    part = lane // experts % 3
    expert = lane % experts
    dense = jnp.zeros((lanes, rows), F32)
    for m in range(routes.shape[2]):
        for i in range(len(outs)):
            here = group == m * len(outs) + i
            chosen = routes[0, :, m, i * rows : (i + 1) * rows]
            weight = gates[0, :, m, i * rows : (i + 1) * rows]
            for k in range(chosen.shape[0]):
                named = here & (chosen[k : k + 1, :] == expert)
                dense = dense + jnp.where(named, weight[k : k + 1, :], 0.0)
    high = dense.astype(BF16)
    rest = dense - high.astype(F32)
    middle = rest.astype(BF16)
    low = (rest - middle.astype(F32)).astype(BF16)
    pieces = [x.astype(F32) for x in (high, middle, low)]
    chosen = jnp.where(part == 0, pieces[0], jnp.where(part == 1, pieces[1], pieces[2]))
    columns[...] = jnp.transpose(chosen).astype(BF16)
    outs[0][:, 2 * depth :] = columns[...]
    for copy in copies:
        copy.wait()


def payloads(routes, gates, inputs, cot_early, experts):
    half, depth = inputs.shape[2] // 2, inputs.shape[3]
    lanes = 2 * 2 * 3 * experts
    lanes += -lanes % LANES
    small = pl.BlockSpec(memory_space=pltpu.VMEM)
    large = pl.BlockSpec(memory_space=pltpu.HBM)
    return pl.pallas_call(
        functools.partial(payload_kernel, experts, half),
        in_specs=[small, small, large, large],
        out_specs=[small, small],
        out_shape=[
            jax.ShapeDtypeStruct((half, 2 * depth + lanes), BF16),
            jax.ShapeDtypeStruct((half, 2 * depth), BF16),
        ],
        scratch_shapes=[pltpu.VMEM((half, lanes), BF16), pltpu.SemaphoreType.DMA((4,))],
        compiler_params=pltpu.CompilerParams(vmem_limit_bytes=VMEM_BYTES),
        name="payloads",
    )(jnp.moveaxis(routes, 3, 1), jnp.moveaxis(gates, 3, 1), inputs, cot_early)


def after(x, *done):
    return lax.optimization_barrier((x, done))[0]


def on_device(inputs, routes, gates, cot_early, head_grad, w_gate, w_up, w_down):
    w_gate, w_up, w_down = w_gate[0], w_up[0], w_down[0]
    grid = Grid(lax.axis_size("expert"))
    me = lax.axis_index("expert")
    local, depth, width = w_gate.shape
    experts = local * lax.axis_size("expert")
    first_in, second_in = inputs[0, 0], inputs[0, 1]
    first_cot = cot_early[0]
    tokens = first_in.shape[0]
    half = tokens // 2
    halves = [slice(0, half), slice(half, tokens)]
    is_first = lax.axis_index("section") == 0
    everyone = half * grid.nz * grid.ny
    a0, b0 = payloads(routes, gates, inputs, cot_early, experts)
    lanes = a0.shape[1] - 2 * depth
    me = jnp.full((1,), lax.axis_index("expert"), jnp.int32)
    weights = (w_gate, w_up, w_down)

    def fuse(blocks):
        return jnp.concatenate(blocks, axis=0)

    def mix(*values):
        return [part for group in zip(*values) for part in group]

    def rows_of(m, part, x, c):
        results = expert_rows(
            everyone, (x[0], c[0], gate_blocks), (x[1], c[1], (half, half, (0, 2 * depth))),
            ((2 * m + part) * 3 * experts, experts), lanes, me, weights, grid.ny,
        )
        for kept, value in zip((xs, cs, dgs, dus, hs), results):
            kept.append(value)
        return results[5:]

    xs, cs, dgs, dus, hs = [], [], [], [], []

    def early_rows(part, blocks):
        return rows_of(0, part, (blocks, (half, half, (0, 0))), (blocks, (half, half, (0, depth))))

    def late_rows(part, blocks):
        x = (second_blocks, (half, tokens, (halves[part].start, 0)))
        return rows_of(1, part, x, (blocks, (half, half, (0, 0))))

    def early_grad(part, total):
        rows = halves[part]
        grad = (first_cot[rows].astype(F32) + total).astype(BF16)
        return grad, jnp.where(is_first, head_grad[rows], grad)

    last = {"z": (), "y": ()}

    def turn(link, move, *x):
        x = after(x, last[link])
        last[link] = move(*x)
        return last[link]

    straight = lambda link, move, *x: move(*x)
    a, b = halves
    along_z = lambda x: grid.along_z(x)[1:]
    ya, yb, yx = grid.near(a0), grid.near(b0), grid.near(second_in)
    za = turn("z", along_z, a0)
    fa = grid.near(after(fuse(za), ya, yb, yx))
    zb = turn("z", along_z, b0)
    gate_blocks = [a0] + za + mix(ya, fa)
    fb = grid.near(fuse(zb))
    zx = turn("z", along_z, second_in)
    back_a = early_rows(0, gate_blocks)
    own_a, sums_a = grid.reduce_y(back_a)
    back_b = early_rows(1, after([b0] + zb + mix(yb, fb), zx))
    total_a = grid.reduce_z(own_a, sums_a, turn)
    fx = grid.near(after(fuse(zx), back_b))
    own_b, sums_b = grid.reduce_y(back_b)
    early_a, sent_a = early_grad(0, total_a)
    move_down = lambda *x: [grid.move_down(x[0], k) for k in grid.along]
    down_a = turn("z", move_down, after(sent_a, fx))
    second_blocks = [second_in] + zx + mix(yx, fx)
    total_b = grid.reduce_z(own_b, sums_b, straight)
    fa = grid.near(fuse(down_a))
    early_b, sent_b = early_grad(1, total_b)
    down_b = turn("z", move_down, sent_b)
    late_back_a = late_rows(0, down_a + fa)
    fb = grid.near(fuse(down_b))
    own_a, sums_a = grid.reduce_y(late_back_a)
    late_back_b = late_rows(1, down_b + fb)
    total_a = grid.reduce_z(own_a, sums_a, turn)
    own_b, sums_b = grid.reduce_y(late_back_b)
    total_b = grid.reduce_z(own_b, sums_b, turn)
    grad_late_a = (down_a[0].astype(F32) + total_a).astype(BF16)
    grad_late_b = (down_b[0].astype(F32) + total_b).astype(BF16)
    grad_gate = outer(after(xs, late_back_b, sums_a), dgs, local, depth, width, "outer_gate")
    grad_up = outer(after(xs, sums_b), dus, local, depth, width, "outer_up")
    grad_down = outer(after(hs, sums_b), cs, local, width, depth, "outer_down")
    grad_early = jnp.concatenate([early_a, early_b], axis=0)
    grad_late = jnp.concatenate([grad_late_a, grad_late_b], axis=0)
    return (grad_early[None], grad_late[None], grad_gate[None], grad_up[None], grad_down[None])


def solution(mesh):
    in_specs = (
        P("section", None, "expert", None),
        P("section", None, "expert", None),
        P("section", None, "expert", None),
        P("section", "expert", None),
        P("expert", None),
        P("section", "expert", None, None),
        P("section", "expert", None, None),
        P("section", "expert", None, None),
    )
    out_specs = (
        P("section", "expert", None),
        P("section", "expert", None),
        P("section", "expert", None, None),
        P("section", "expert", None, None),
        P("section", "expert", None, None),
    )
    return jax.shard_map(
        on_device, mesh=mesh, in_specs=in_specs, out_specs=out_specs, check_vma=False
    )
```

```python
import functools

import jax
import jax.numpy as jnp
from jax import lax
from jax.experimental import pallas as pl
from jax.experimental.pallas import tpu as pltpu
from jax.sharding import PartitionSpec as P

LANES = 128
VMEM_BYTES = 60 * 1024 * 1024
OUTER_VMEM_BYTES = 24 * 1024 * 1024
NT = (((1,), (1,)), ((), ()))
TN = (((0,), (0,)), ((), ()))
BF16 = jnp.bfloat16
F32 = jnp.float32


def dot(a, b, dims=(((1,), (0,)), ((), ()))):
    return lax.dot_general(a, b, dims, preferred_element_type=F32)


class Grid:
    def __init__(self, count):
        self.ny = max(d for d in range(1, count + 1) if count % d == 0 and d * d <= count)
        self.nz = count // self.ny
        self.far = sorted(range(1, self.nz), key=lambda k: (min(k, self.nz - k), k))
        self.along = [0] + self.far

    def pairs(self, dz, dy):
        return [
            (z * self.ny + y, (z + dz) % self.nz * self.ny + (y + dy) % self.ny)
            for z in range(self.nz)
            for y in range(self.ny)
        ]

    def move(self, x, dz, dy):
        with jax.named_scope(f"z{dz}y{dy}"):
            return lax.ppermute(x, "expert", self.pairs(dz, dy))

    def move_down(self, x, dz):
        sections, count = lax.axis_size("section"), lax.axis_size("expert")
        pairs = [
            (s * count + a, (s - 1) % sections * count + b)
            for s in range(sections)
            for a, b in self.pairs(dz, 0)
        ]
        with jax.named_scope(f"down_z{dz}"):
            return lax.ppermute(x, ("section", "expert"), pairs)

    def along_z(self, x):
        return [x] + [self.move(x, k, 0) for k in self.far]

    def near(self, x):
        return [self.move(x, 0, j) for j in range(1, self.ny)]

    def reduce_y(self, parts):
        move = lambda *x: [self.move(part, 0, -j) for j, part in enumerate(x, 1)]
        summed = parts[0].astype(F32)
        for moved in move(*parts[1:]):
            summed = summed + moved.astype(F32)
        rows = summed.shape[0] // self.nz
        own = summed[:rows]
        return own, [summed[i * rows : (i + 1) * rows].astype(BF16) for i in range(1, self.nz)]

    def reduce_z(self, own, blocks, turn):
        move = lambda *x: [self.move(block, -k, 0) for k, block in zip(self.far, x)]
        for moved in turn("z", move, *blocks):
            own = own + moved.astype(F32)
        return own


def on_core(kernel, name, flops, index, operands, out_shape, scratch):
    hbm = pl.BlockSpec(memory_space=pltpu.HBM)
    return pl.pallas_call(
        kernel,
        in_specs=[pl.BlockSpec(memory_space=pltpu.SMEM)] * len(index) + [hbm] * len(operands),
        out_specs=[hbm] * len(out_shape),
        out_shape=out_shape,
        scratch_shapes=scratch,
        compiler_params=pltpu.CompilerParams(vmem_limit_bytes=VMEM_BYTES),
        cost_estimate=pl.CostEstimate(flops=int(flops), bytes_accessed=0, transcendentals=0),
        name=name,
    )(*index, *operands)


def join(refs, whole, place, sem):
    rows, block, at = place
    copies, start = [], 0
    for ref in refs:
        for first in range(at[0], ref.shape[0], block):
            copies.append(
                pltpu.make_async_copy(
                    ref.at[first : first + rows, at[1] : at[1] + whole.shape[1]],
                    whole.at[start : start + rows, :],
                    sem.at[len(copies)],
                )
            )
            start += rows
    return copies


def tiles(size):
    tile = min(256, size)
    return [slice(i, i + tile) for i in range(0, size, tile)]


def rows_kernel(counts, places, lane, count, me, *refs):
    refs = list(refs)
    take = lambda n: [refs.pop(0) for _ in range(n)]
    x_refs, c_refs, g_refs = (take(n) for n in counts)
    weights_hbm = take(3)
    x_hbm, c_hbm = take(2)
    values_hbm, outs = take(3), take(count)
    weights, values = take(3), take(3)
    x, c, g, gate, up, back, total_out, x_sem, c_sem, g_sem, w_sem, v_sem, out_sem = refs
    gate_w, up_w, down_w = weights
    grad_gate, grad_up, hidden = values
    local, depth, width = gate_w.shape
    rows = outs[0].shape[0]
    x_copies = join(x_refs, x, places[0], x_sem)
    c_copies = join(c_refs, c, places[1], c_sem)
    g_copies = join(g_refs, g, places[2], g_sem)
    queue = [
        pltpu.make_async_copy(weights_hbm[i].at[e], weights[i].at[e], w_sem.at[i * local + e])
        for e in range(local)
        for i in (2, 0, 1)
    ]

    def arrived(position):
        if position + 2 < len(queue):
            queue[position + 2].start()
        queue[position].wait()

    for copy in c_copies + g_copies + queue[:1] + x_copies + queue[1:2]:
        copy.start()
    for copy in c_copies + g_copies:
        copy.wait()
    writes = []

    def write(*copy):
        writes.append(pltpu.make_async_copy(*copy))
        writes[-1].start()

    experts = lane[1]
    at_lane = lax.broadcasted_iota(jnp.int32, (g.shape[1], tiles(width)[0].stop), 0)
    for e in range(local):
        arrived(3 * e)
        first = lane[0] + me[0] * local + e
        mine = (at_lane == first) | (at_lane == first + experts) | (at_lane == first + 2 * experts)
        weight = dot(g[...], mine.astype(F32).astype(BF16))
        grads = [dot(c[...], down_w[e, f, :], NT) * weight for f in tiles(width)]
        if e == 0:
            for copy in x_copies:
                copy.wait()
        arrived(3 * e + 1)
        if e == local - 1:
            write(x, x_hbm, v_sem.at[3])
            write(c, c_hbm, v_sem.at[4])
        for f in tiles(width):
            gate[:, f] = dot(x[...], gate_w[e, :, f])
        arrived(3 * e + 2)
        for f in tiles(width):
            up[:, f] = dot(x[...], up_w[e, :, f])
        for f, grad_hidden in zip(tiles(width), grads):
            at = slice(e * width + f.start, e * width + f.stop)
            gate_value, up_value = gate[:, f], up[:, f]
            sigmoid_value = jax.nn.sigmoid(gate_value)
            swished = gate_value * sigmoid_value
            derivative = sigmoid_value * (1.0 + gate_value * (1.0 - sigmoid_value))
            hidden[:, at] = (swished * up_value * weight).astype(BF16)
            grad_gate[:, at] = (grad_hidden * up_value * derivative).astype(BF16)
            grad_up[:, at] = (grad_hidden * swished).astype(BF16)
        columns = slice(e * width, (e + 1) * width)
        if e == local - 1:
            for i in range(3):
                write(values[i], values_hbm[i], v_sem.at[i])
        for d in tiles(depth):
            total = dot(grad_gate[:, columns], gate_w[e, d, :], NT)
            total = total + dot(grad_up[:, columns], up_w[e, d, :], NT)
            if e:
                total = total + back[:, d]
            if e < local - 1:
                back[:, d] = total
                continue
            total_out[:, d] = total.astype(BF16)
            if d.stop in (depth // 2, depth):
                side = slice(d.stop - depth // 2, d.stop)
                for j, out in enumerate(outs):
                    sem = out_sem.at[j, d.stop // depth]
                    write(total_out.at[j * rows : (j + 1) * rows, side], out.at[:, side], sem)
    for copy in writes:
        copy.wait()


def expert_rows(tokens, blocks, places, lane, lanes, me, weights, count):
    local, depth, width = weights[0].shape
    value = (tokens, local * width)
    return on_core(
        functools.partial(rows_kernel, [len(x) for x in blocks], places, lane, count),
        "expert_rows",
        10 * tokens * depth * local * width,
        [me],
        [*blocks[0], *blocks[1], *blocks[2], *weights],
        [jax.ShapeDtypeStruct((tokens, depth), BF16)] * 2
        + [jax.ShapeDtypeStruct(value, BF16)] * 3
        + [jax.ShapeDtypeStruct((tokens // count, depth), BF16)] * count,
        [pltpu.VMEM(w.shape, BF16) for w in weights]
        + [pltpu.VMEM(value, BF16)] * 3
        + [pltpu.VMEM((tokens, depth), BF16)] * 2
        + [pltpu.VMEM((tokens, lanes), BF16)]
        + [pltpu.VMEM((tokens, width), F32)] * 2
        + [pltpu.VMEM((tokens, depth), F32), pltpu.VMEM((tokens, depth), BF16)]
        + [pltpu.SemaphoreType.DMA((tokens // place[0],)) for place in places]
        + [pltpu.SemaphoreType.DMA((3 * local,)), pltpu.SemaphoreType.DMA((5,))]
        + [pltpu.SemaphoreType.DMA((count, 2))],
    )


def outer_kernel(pieces, count, *refs):
    lefts, rights, (*outs, right) = refs[:pieces], refs[pieces : (1 + count) * pieces], refs[(1 + count) * pieces :]
    local, rows, columns = outs[0].shape
    wide = right.shape[1] // count
    for i in range(count):
        start = 0
        for ref in rights[i * pieces : (i + 1) * pieces]:
            right[start : start + ref.shape[0], i * wide : (i + 1) * wide] = ref[...]
            start += ref.shape[0]
    for m in tiles(lefts[0].shape[1]):
        left = jnp.concatenate([ref[:, m] for ref in lefts], axis=0)
        product = dot(left, right[...], TN).astype(BF16)
        if lefts[0].shape[1] == rows:
            for i, out in enumerate(outs):
                for e in range(local):
                    at = i * wide + e * columns
                    out[e, m, :] = product[:, at : at + columns]
        else:
            at = m.start % rows
            outs[0][m.start // rows, at : at + m.stop - m.start, :] = product


def outer(lefts, rights, local, rows, columns, name):
    tokens, count = sum(x.shape[0] for x in lefts), len(rights)
    spec = pl.BlockSpec(memory_space=pltpu.VMEM)
    return pl.pallas_call(
        functools.partial(outer_kernel, len(lefts), count),
        in_specs=[spec] * ((1 + count) * len(lefts)),
        out_specs=[spec] * count,
        out_shape=[jax.ShapeDtypeStruct((local, rows, columns), BF16)] * count,
        scratch_shapes=[pltpu.VMEM((tokens, count * rights[0][0].shape[1]), BF16)],
        compiler_params=pltpu.CompilerParams(vmem_limit_bytes=OUTER_VMEM_BYTES),
        cost_estimate=pl.CostEstimate(
            flops=2 * count * tokens * local * rows * columns, bytes_accessed=0, transcendentals=0
        ),
        name=name,
    )(*lefts, *sum(rights, []))


def payload_kernel(experts, half, routes, gates, x_in, c_in, *refs):
    *outs, columns, sems = refs
    rows, depth = half, x_in.shape[-1]
    copies = []
    for i, out in enumerate(outs):
        from_rows = slice(i * rows, (i + 1) * rows)
        for j, source in enumerate((x_in.at[0, 0], c_in.at[0])):
            copies.append(
                pltpu.make_async_copy(
                    source.at[from_rows, :],
                    out.at[:, j * depth : (j + 1) * depth],
                    sems.at[len(copies)],
                )
            )
    for copy in copies:
        copy.start()
    lanes = columns.shape[1]
    lane = lax.broadcasted_iota(jnp.int32, (lanes, rows), 0)
    group = lane // (3 * experts)
    part = lane // experts % 3
    expert = lane % experts
    dense = jnp.zeros((lanes, rows), F32)
    for m in range(routes.shape[2]):
        for i in range(len(outs)):
            here = group == m * len(outs) + i
            chosen = routes[0, :, m, i * rows : (i + 1) * rows]
            weight = gates[0, :, m, i * rows : (i + 1) * rows]
            for k in range(chosen.shape[0]):
                named = here & (chosen[k : k + 1, :] == expert)
                dense = dense + jnp.where(named, weight[k : k + 1, :], 0.0)
    high = dense.astype(BF16)
    rest = dense - high.astype(F32)
    middle = rest.astype(BF16)
    low = (rest - middle.astype(F32)).astype(BF16)
    pieces = [x.astype(F32) for x in (high, middle, low)]
    chosen = jnp.where(part == 0, pieces[0], jnp.where(part == 1, pieces[1], pieces[2]))
    columns[...] = jnp.transpose(chosen).astype(BF16)
    outs[0][:, 2 * depth :] = columns[...]
    for copy in copies:
        copy.wait()


def payloads(routes, gates, inputs, cot_early, experts):
    half, depth = inputs.shape[2] // 2, inputs.shape[3]
    lanes = 2 * 2 * 3 * experts
    lanes += -lanes % LANES
    small = pl.BlockSpec(memory_space=pltpu.VMEM)
    large = pl.BlockSpec(memory_space=pltpu.HBM)
    return pl.pallas_call(
        functools.partial(payload_kernel, experts, half),
        in_specs=[small, small, large, large],
        out_specs=[small, small],
        out_shape=[
            jax.ShapeDtypeStruct((half, 2 * depth + lanes), BF16),
            jax.ShapeDtypeStruct((half, 2 * depth), BF16),
        ],
        scratch_shapes=[pltpu.VMEM((half, lanes), BF16), pltpu.SemaphoreType.DMA((4,))],
        compiler_params=pltpu.CompilerParams(vmem_limit_bytes=VMEM_BYTES),
        name="payloads",
    )(jnp.moveaxis(routes, 3, 1), jnp.moveaxis(gates, 3, 1), inputs, cot_early)


def after(x, *done):
    return lax.optimization_barrier((x, done))[0]


def on_device(inputs, routes, gates, cot_early, head_grad, w_gate, w_up, w_down):
    w_gate, w_up, w_down = w_gate[0], w_up[0], w_down[0]
    grid = Grid(lax.axis_size("expert"))
    me = lax.axis_index("expert")
    local, depth, width = w_gate.shape
    experts = local * lax.axis_size("expert")
    first_in, second_in = inputs[0, 0], inputs[0, 1]
    first_cot = cot_early[0]
    tokens = first_in.shape[0]
    half = tokens // 2
    halves = [slice(0, half), slice(half, tokens)]
    is_first = lax.axis_index("section") == 0
    everyone = half * grid.nz * grid.ny
    a0, b0 = payloads(routes, gates, inputs, cot_early, experts)
    lanes = a0.shape[1] - 2 * depth
    me = jnp.full((1,), lax.axis_index("expert"), jnp.int32)
    weights = (w_gate, w_up, w_down)

    def fuse(blocks):
        return jnp.concatenate(blocks, axis=0)

    def mix(*values):
        return [part for group in zip(*values) for part in group]

    def rows_of(m, part, x, c):
        results = expert_rows(
            everyone, (x[0], c[0], gate_blocks), (x[1], c[1], (half, half, (0, 2 * depth))),
            ((2 * m + part) * 3 * experts, experts), lanes, me, weights, grid.ny,
        )
        for kept, value in zip((xs, cs, dgs, dus, hs), results):
            kept.append(value)
        return results[5:]

    xs, cs, dgs, dus, hs = [], [], [], [], []

    def early_rows(part, blocks):
        return rows_of(0, part, (blocks, (half, half, (0, 0))), (blocks, (half, half, (0, depth))))

    def late_rows(part, blocks):
        x = (second_blocks, (half, tokens, (halves[part].start, 0)))
        return rows_of(1, part, x, (blocks, (half, half, (0, 0))))

    def early_grad(part, total):
        rows = halves[part]
        grad = (first_cot[rows].astype(F32) + total).astype(BF16)
        return grad, jnp.where(is_first, head_grad[rows], grad)

    last = {"z": (), "y": ()}

    def turn(link, move, *x):
        x = after(x, last[link])
        last[link] = move(*x)
        return last[link]

    straight = lambda link, move, *x: move(*x)
    a, b = halves
    along_z = lambda x: grid.along_z(x)[1:]
    ya, yb, yx = grid.near(a0), grid.near(b0), grid.near(second_in)
    za = turn("z", along_z, a0)
    fa = grid.near(after(fuse(za), ya, yb, yx))
    zb = turn("z", along_z, b0)
    gate_blocks = [a0] + za + mix(ya, fa)
    fb = grid.near(fuse(zb))
    zx = turn("z", along_z, second_in)
    back_a = early_rows(0, gate_blocks)
    own_a, sums_a = grid.reduce_y(back_a)
    back_b = early_rows(1, after([b0] + zb + mix(yb, fb), zx))
    total_a = grid.reduce_z(own_a, sums_a, turn)
    fx = grid.near(after(fuse(zx), back_b))
    own_b, sums_b = grid.reduce_y(back_b)
    early_a, sent_a = early_grad(0, total_a)
    move_down = lambda *x: [grid.move_down(x[0], k) for k in grid.along]
    down_a = turn("z", move_down, after(sent_a, fx))
    second_blocks = [second_in] + zx + mix(yx, fx)
    total_b = grid.reduce_z(own_b, sums_b, straight)
    fa = grid.near(fuse(down_a))
    early_b, sent_b = early_grad(1, total_b)
    down_b = move_down(sent_b)
    late_back_a = late_rows(0, down_a + fa)
    fb = grid.near(fuse(down_b))
    own_a, sums_a = grid.reduce_y(late_back_a)
    late_back_b = late_rows(1, down_b + fb)
    total_a = grid.reduce_z(own_a, sums_a, straight)
    own_b, sums_b = grid.reduce_y(late_back_b)
    total_b = grid.reduce_z(own_b, sums_b, straight)
    grad_late_a = (down_a[0].astype(F32) + total_a).astype(BF16)
    grad_late_b = (down_b[0].astype(F32) + total_b).astype(BF16)
    (grad_down,) = outer(after(hs, late_back_a, late_back_b, sums_b), [cs], local, width, depth, "outer_down")
    grad_gate, grad_up = outer(after(xs, sums_a, total_b), [dgs, dus], local, depth, width, "outer_inputs")
    grad_early = jnp.concatenate([early_a, early_b], axis=0)
    grad_late = jnp.concatenate([grad_late_a, grad_late_b], axis=0)
    return (grad_early[None], grad_late[None], grad_gate[None], grad_up[None], grad_down[None])


def solution(mesh):
    in_specs = (
        P("section", None, "expert", None),
        P("section", None, "expert", None),
        P("section", None, "expert", None),
        P("section", "expert", None),
        P("expert", None),
        P("section", "expert", None, None),
        P("section", "expert", None, None),
        P("section", "expert", None, None),
    )
    out_specs = (
        P("section", "expert", None),
        P("section", "expert", None),
        P("section", "expert", None, None),
        P("section", "expert", None, None),
        P("section", "expert", None, None),
    )
    return jax.shard_map(
        on_device, mesh=mesh, in_specs=in_specs, out_specs=out_specs, check_vma=False
    )
```

```python
import functools

import jax
import jax.numpy as jnp
from jax import lax
from jax.experimental import pallas as pl
from jax.experimental.pallas import tpu as pltpu
from jax.sharding import PartitionSpec as P

LANES = 128
VMEM_BYTES = 60 * 1024 * 1024
OUTER_VMEM_BYTES = 24 * 1024 * 1024
NT = (((1,), (1,)), ((), ()))
TN = (((0,), (0,)), ((), ()))
BF16 = jnp.bfloat16
F32 = jnp.float32


def dot(a, b, dims=(((1,), (0,)), ((), ()))):
    return lax.dot_general(a, b, dims, preferred_element_type=F32)


class Grid:
    def __init__(self, count):
        self.ny = max(d for d in range(1, count + 1) if count % d == 0 and d * d <= count)
        self.nz = count // self.ny
        self.far = sorted(range(1, self.nz), key=lambda k: (min(k, self.nz - k), k))
        self.along = [0] + self.far

    def pairs(self, dz, dy):
        return [
            (z * self.ny + y, (z + dz) % self.nz * self.ny + (y + dy) % self.ny)
            for z in range(self.nz)
            for y in range(self.ny)
        ]

    def move(self, x, dz, dy):
        with jax.named_scope(f"z{dz}y{dy}"):
            return lax.ppermute(x, "expert", self.pairs(dz, dy))

    def move_down(self, x, dz):
        sections, count = lax.axis_size("section"), lax.axis_size("expert")
        pairs = [
            (s * count + a, (s - 1) % sections * count + b)
            for s in range(sections)
            for a, b in self.pairs(dz, 0)
        ]
        with jax.named_scope(f"down_z{dz}"):
            return lax.ppermute(x, ("section", "expert"), pairs)

    def along_z(self, x):
        return [x] + [self.move(x, k, 0) for k in self.far]

    def near(self, x):
        return [self.move(x, 0, j) for j in range(1, self.ny)]

    def reduce_y(self, parts):
        move = lambda *x: [self.move(part, 0, -j) for j, part in enumerate(x, 1)]
        summed = parts[0].astype(F32)
        for moved in move(*parts[1:]):
            summed = summed + moved.astype(F32)
        rows = summed.shape[0] // self.nz
        own = summed[:rows]
        return own, [summed[i * rows : (i + 1) * rows].astype(BF16) for i in range(1, self.nz)]

    def reduce_z(self, own, blocks, turn):
        move = lambda *x: [self.move(block, -k, 0) for k, block in zip(self.far, x)]
        for moved in turn("z", move, *blocks):
            own = own + moved.astype(F32)
        return own


def on_core(kernel, name, flops, index, operands, out_shape, scratch):
    hbm = pl.BlockSpec(memory_space=pltpu.HBM)
    return pl.pallas_call(
        kernel,
        in_specs=[pl.BlockSpec(memory_space=pltpu.SMEM)] * len(index) + [hbm] * len(operands),
        out_specs=[hbm] * len(out_shape),
        out_shape=out_shape,
        scratch_shapes=scratch,
        compiler_params=pltpu.CompilerParams(vmem_limit_bytes=VMEM_BYTES),
        cost_estimate=pl.CostEstimate(flops=int(flops), bytes_accessed=0, transcendentals=0),
        name=name,
    )(*index, *operands)


def join(refs, whole, place, sem):
    rows, block, at = place
    copies, start = [], 0
    for ref in refs:
        for first in range(at[0], ref.shape[0], block):
            copies.append(
                pltpu.make_async_copy(
                    ref.at[first : first + rows, at[1] : at[1] + whole.shape[1]],
                    whole.at[start : start + rows, :],
                    sem.at[len(copies)],
                )
            )
            start += rows
    return copies


def tiles(size):
    tile = min(256, size)
    return [slice(i, i + tile) for i in range(0, size, tile)]


def rows_kernel(counts, places, lane, count, me, *refs):
    refs = list(refs)
    take = lambda n: [refs.pop(0) for _ in range(n)]
    x_refs, c_refs, g_refs = (take(n) for n in counts)
    weights_hbm = take(3)
    x_hbm, c_hbm = take(2)
    values_hbm, outs = take(3), take(count)
    weights, values = take(3), take(3)
    x, c, g, gate, up, total_out, x_sem, c_sem, g_sem, w_sem, v_sem, out_sem = refs
    gate_w, up_w, down_w = weights
    grad_gate, grad_up, hidden = values
    local, depth, width = gate_w.shape
    rows = outs[0].shape[0]
    x_copies = join(x_refs, x, places[0], x_sem)
    c_copies = join(c_refs, c, places[1], c_sem)
    g_copies = join(g_refs, g, places[2], g_sem)
    queue = [
        pltpu.make_async_copy(weights_hbm[i].at[e], weights[i].at[e], w_sem.at[i * local + e])
        for e in range(local)
        for i in (2, 0, 1)
    ]

    def arrived(position):
        if position + 2 < len(queue):
            queue[position + 2].start()
        queue[position].wait()

    for copy in c_copies + g_copies + queue[:1] + x_copies + queue[1:2]:
        copy.start()
    for copy in c_copies + g_copies:
        copy.wait()
    writes = []

    def write(*copy):
        writes.append(pltpu.make_async_copy(*copy))
        writes[-1].start()

    experts = lane[1]
    at_lane = lax.broadcasted_iota(jnp.int32, (g.shape[1], tiles(width)[0].stop), 0)
    for e in range(local):
        arrived(3 * e)
        first = lane[0] + me[0] * local + e
        mine = (at_lane == first) | (at_lane == first + experts) | (at_lane == first + 2 * experts)
        weight = dot(g[...], mine.astype(F32).astype(BF16))
        grads = [dot(c[...], down_w[e, f, :], NT) * weight for f in tiles(width)]
        if e == 0:
            for copy in x_copies:
                copy.wait()
        arrived(3 * e + 1)
        if e == local - 1:
            write(x, x_hbm, v_sem.at[3])
            write(c, c_hbm, v_sem.at[4])
        for f in tiles(width):
            gate[:, f] = dot(x[...], gate_w[e, :, f])
        arrived(3 * e + 2)
        for f in tiles(width):
            up[:, f] = dot(x[...], up_w[e, :, f])
        for f, grad_hidden in zip(tiles(width), grads):
            at = slice(e * width + f.start, e * width + f.stop)
            gate_value, up_value = gate[:, f], up[:, f]
            sigmoid_value = jax.nn.sigmoid(gate_value)
            swished = gate_value * sigmoid_value
            derivative = sigmoid_value * (1.0 + gate_value * (1.0 - sigmoid_value))
            hidden[:, at] = (swished * up_value * weight).astype(BF16)
            grad_gate[:, at] = (grad_hidden * up_value * derivative).astype(BF16)
            grad_up[:, at] = (grad_hidden * swished).astype(BF16)
        columns = slice(e * width, (e + 1) * width)
        if e == local - 1:
            for i in range(3):
                write(values[i], values_hbm[i], v_sem.at[i])
        for d in tiles(depth) if e == local - 1 else ():
            total = None
            for part in range(local):
                columns = slice(part * width, (part + 1) * width)
                for grad, weight_of in ((grad_gate, gate_w), (grad_up, up_w)):
                    term = dot(grad[:, columns], weight_of[part, d, :], NT)
                    total = term if total is None else total + term
            total_out[:, d] = total.astype(BF16)
            if d.stop in (depth // 2, depth):
                side = slice(d.stop - depth // 2, d.stop)
                for j, out in enumerate(outs):
                    sem = out_sem.at[j, d.stop // depth]
                    write(total_out.at[j * rows : (j + 1) * rows, side], out.at[:, side], sem)
    for copy in writes:
        copy.wait()


def expert_rows(tokens, blocks, places, lane, lanes, me, weights, count):
    local, depth, width = weights[0].shape
    value = (tokens, local * width)
    return on_core(
        functools.partial(rows_kernel, [len(x) for x in blocks], places, lane, count),
        "expert_rows",
        10 * tokens * depth * local * width,
        [me],
        [*blocks[0], *blocks[1], *blocks[2], *weights],
        [jax.ShapeDtypeStruct((tokens, depth), BF16)] * 2
        + [jax.ShapeDtypeStruct(value, BF16)] * 3
        + [jax.ShapeDtypeStruct((tokens // count, depth), BF16)] * count,
        [pltpu.VMEM(w.shape, BF16) for w in weights]
        + [pltpu.VMEM(value, BF16)] * 3
        + [pltpu.VMEM((tokens, depth), BF16)] * 2
        + [pltpu.VMEM((tokens, lanes), BF16)]
        + [pltpu.VMEM((tokens, width), F32)] * 2
        + [pltpu.VMEM((tokens, depth), BF16)]
        + [pltpu.SemaphoreType.DMA((tokens // place[0],)) for place in places]
        + [pltpu.SemaphoreType.DMA((3 * local,)), pltpu.SemaphoreType.DMA((5,))]
        + [pltpu.SemaphoreType.DMA((count, 2))],
    )


def outer_kernel(pieces, count, *refs):
    lefts, rights, (*outs, right) = refs[:pieces], refs[pieces : (1 + count) * pieces], refs[(1 + count) * pieces :]
    local, rows, columns = outs[0].shape
    wide = right.shape[1] // count
    for i in range(count):
        start = 0
        for ref in rights[i * pieces : (i + 1) * pieces]:
            right[start : start + ref.shape[0], i * wide : (i + 1) * wide] = ref[...]
            start += ref.shape[0]
    for m in tiles(lefts[0].shape[1]):
        left = jnp.concatenate([ref[:, m] for ref in lefts], axis=0)
        product = dot(left, right[...], TN).astype(BF16)
        if lefts[0].shape[1] == rows:
            for i, out in enumerate(outs):
                for e in range(local):
                    at = i * wide + e * columns
                    out[e, m, :] = product[:, at : at + columns]
        else:
            at = m.start % rows
            outs[0][m.start // rows, at : at + m.stop - m.start, :] = product


def outer(lefts, rights, local, rows, columns, name):
    tokens, count = sum(x.shape[0] for x in lefts), len(rights)
    spec = pl.BlockSpec(memory_space=pltpu.VMEM)
    return pl.pallas_call(
        functools.partial(outer_kernel, len(lefts), count),
        in_specs=[spec] * ((1 + count) * len(lefts)),
        out_specs=[spec] * count,
        out_shape=[jax.ShapeDtypeStruct((local, rows, columns), BF16)] * count,
        scratch_shapes=[pltpu.VMEM((tokens, count * rights[0][0].shape[1]), BF16)],
        compiler_params=pltpu.CompilerParams(vmem_limit_bytes=OUTER_VMEM_BYTES),
        cost_estimate=pl.CostEstimate(
            flops=2 * count * tokens * local * rows * columns, bytes_accessed=0, transcendentals=0
        ),
        name=name,
    )(*lefts, *sum(rights, []))


def payload_kernel(experts, half, routes, gates, x_in, c_in, *refs):
    *outs, columns, sems = refs
    rows, depth = half, x_in.shape[-1]
    copies = []
    for i, out in enumerate(outs):
        from_rows = slice(i * rows, (i + 1) * rows)
        for j, source in enumerate((x_in.at[0, 0], c_in.at[0])):
            copies.append(
                pltpu.make_async_copy(
                    source.at[from_rows, :],
                    out.at[:, j * depth : (j + 1) * depth],
                    sems.at[len(copies)],
                )
            )
    for copy in copies:
        copy.start()
    lanes = columns.shape[1]
    lane = lax.broadcasted_iota(jnp.int32, (lanes, rows), 0)
    group = lane // (3 * experts)
    part = lane // experts % 3
    expert = lane % experts
    dense = jnp.zeros((lanes, rows), F32)
    for m in range(routes.shape[2]):
        for i in range(len(outs)):
            here = group == m * len(outs) + i
            chosen = routes[0, :, m, i * rows : (i + 1) * rows]
            weight = gates[0, :, m, i * rows : (i + 1) * rows]
            for k in range(chosen.shape[0]):
                named = here & (chosen[k : k + 1, :] == expert)
                dense = dense + jnp.where(named, weight[k : k + 1, :], 0.0)
    high = dense.astype(BF16)
    rest = dense - high.astype(F32)
    middle = rest.astype(BF16)
    low = (rest - middle.astype(F32)).astype(BF16)
    pieces = [x.astype(F32) for x in (high, middle, low)]
    chosen = jnp.where(part == 0, pieces[0], jnp.where(part == 1, pieces[1], pieces[2]))
    columns[...] = jnp.transpose(chosen).astype(BF16)
    outs[0][:, 2 * depth :] = columns[...]
    for copy in copies:
        copy.wait()


def payloads(routes, gates, inputs, cot_early, experts):
    half, depth = inputs.shape[2] // 2, inputs.shape[3]
    lanes = 2 * 2 * 3 * experts
    lanes += -lanes % LANES
    small = pl.BlockSpec(memory_space=pltpu.VMEM)
    large = pl.BlockSpec(memory_space=pltpu.HBM)
    return pl.pallas_call(
        functools.partial(payload_kernel, experts, half),
        in_specs=[small, small, large, large],
        out_specs=[small, small],
        out_shape=[
            jax.ShapeDtypeStruct((half, 2 * depth + lanes), BF16),
            jax.ShapeDtypeStruct((half, 2 * depth), BF16),
        ],
        scratch_shapes=[pltpu.VMEM((half, lanes), BF16), pltpu.SemaphoreType.DMA((4,))],
        compiler_params=pltpu.CompilerParams(vmem_limit_bytes=VMEM_BYTES),
        name="payloads",
    )(jnp.moveaxis(routes, 3, 1), jnp.moveaxis(gates, 3, 1), inputs, cot_early)


def after(x, *done):
    return lax.optimization_barrier((x, done))[0]


def on_device(inputs, routes, gates, cot_early, head_grad, w_gate, w_up, w_down):
    w_gate, w_up, w_down = w_gate[0], w_up[0], w_down[0]
    grid = Grid(lax.axis_size("expert"))
    me = lax.axis_index("expert")
    local, depth, width = w_gate.shape
    experts = local * lax.axis_size("expert")
    first_in, second_in = inputs[0, 0], inputs[0, 1]
    first_cot = cot_early[0]
    tokens = first_in.shape[0]
    half = tokens // 2
    halves = [slice(0, half), slice(half, tokens)]
    is_first = lax.axis_index("section") == 0
    everyone = half * grid.nz * grid.ny
    a0, b0 = payloads(routes, gates, inputs, cot_early, experts)
    lanes = a0.shape[1] - 2 * depth
    me = jnp.full((1,), lax.axis_index("expert"), jnp.int32)
    weights = (w_gate, w_up, w_down)

    def fuse(blocks):
        return jnp.concatenate(blocks, axis=0)

    def mix(*values):
        return [part for group in zip(*values) for part in group]

    def rows_of(m, part, x, c):
        results = expert_rows(
            everyone, (x[0], c[0], gate_blocks), (x[1], c[1], (half, half, (0, 2 * depth))),
            ((2 * m + part) * 3 * experts, experts), lanes, me, weights, grid.ny,
        )
        for kept, value in zip((xs, cs, dgs, dus, hs), results):
            kept.append(value)
        return results[5:]

    xs, cs, dgs, dus, hs = [], [], [], [], []

    def early_rows(part, blocks):
        return rows_of(0, part, (blocks, (half, half, (0, 0))), (blocks, (half, half, (0, depth))))

    def late_rows(part, blocks):
        x = (second_blocks, (half, tokens, (halves[part].start, 0)))
        return rows_of(1, part, x, (blocks, (half, half, (0, 0))))

    def early_grad(part, total):
        rows = halves[part]
        grad = (first_cot[rows].astype(F32) + total).astype(BF16)
        return grad, jnp.where(is_first, head_grad[rows], grad)

    last = {"z": (), "y": ()}

    def turn(link, move, *x):
        x = after(x, last[link])
        last[link] = move(*x)
        return last[link]

    straight = lambda link, move, *x: move(*x)
    a, b = halves
    along_z = lambda x: grid.along_z(x)[1:]
    ya, yx = grid.near(a0), grid.near(second_in)
    za = turn("z", along_z, a0)
    fa = grid.near(after(fuse(za), ya, yx))
    zb = turn("z", along_z, b0)
    gate_blocks = [a0] + za + mix(ya, fa)
    fb = grid.near(fuse([b0] + zb))
    zx = turn("z", along_z, second_in)
    back_a = early_rows(0, gate_blocks)
    own_a, sums_a = grid.reduce_y(back_a)
    back_b = early_rows(1, after([b0] + zb + fb, zx))
    total_a = grid.reduce_z(own_a, sums_a, turn)
    fx = grid.near(after(fuse(zx), back_b))
    own_b, sums_b = grid.reduce_y(back_b)
    early_a, sent_a = early_grad(0, total_a)
    move_down = lambda *x: [grid.move_down(x[0], k) for k in grid.along]
    down_a = turn("z", move_down, after(sent_a, fx))
    second_blocks = [second_in] + zx + mix(yx, fx)
    total_b = grid.reduce_z(own_b, sums_b, straight)
    fa = grid.near(fuse(down_a))
    early_b, sent_b = early_grad(1, total_b)
    down_b = move_down(sent_b)
    late_back_a = late_rows(0, down_a + fa)
    fb = grid.near(fuse(down_b))
    own_a, sums_a = grid.reduce_y(late_back_a)
    late_back_b = late_rows(1, down_b + fb)
    total_a = grid.reduce_z(own_a, sums_a, straight)
    own_b, sums_b = grid.reduce_y(late_back_b)
    total_b = grid.reduce_z(own_b, sums_b, straight)
    grad_late_a = (down_a[0].astype(F32) + total_a).astype(BF16)
    grad_late_b = (down_b[0].astype(F32) + total_b).astype(BF16)
    (grad_down,) = outer(after(hs, late_back_a, late_back_b, sums_b), [cs], local, width, depth, "outer_down")
    grad_gate, grad_up = outer(after(xs, sums_a, total_b), [dgs, dus], local, depth, width, "outer_inputs")
    grad_early = jnp.concatenate([early_a, early_b], axis=0)
    grad_late = jnp.concatenate([grad_late_a, grad_late_b], axis=0)
    return (grad_early[None], grad_late[None], grad_gate[None], grad_up[None], grad_down[None])


def solution(mesh):
    in_specs = (
        P("section", None, "expert", None),
        P("section", None, "expert", None),
        P("section", None, "expert", None),
        P("section", "expert", None),
        P("expert", None),
        P("section", "expert", None, None),
        P("section", "expert", None, None),
        P("section", "expert", None, None),
    )
    out_specs = (
        P("section", "expert", None),
        P("section", "expert", None),
        P("section", "expert", None, None),
        P("section", "expert", None, None),
        P("section", "expert", None, None),
    )
    return jax.shard_map(
        on_device, mesh=mesh, in_specs=in_specs, out_specs=out_specs, check_vma=False
    )
```
